256 devices in a mesh: section: 16 (over z, x_hi), expert: 16 (over y, x_lo, core).
Axes of the slice: x: 4 (x_hi: 2, x_lo: 2; x = x_hi * 2 + x_lo), y: 4, z: 8, core: 2. Of those that a mesh axis runs over, the one named last changes fastest.
Arguments:
- fwd_in: bfloat16 [16, 256, 7168], P('section', 'expert'), may hold values from -6 to 6
- fwd_new: bfloat16 [256, 7168], P('expert'), may hold values from -6 to 6
- grad_in: bfloat16 [16, 256, 7168], P('section', 'expert'), may hold values from -6 to 6
- grad_new: bfloat16 [256, 7168], P('expert'), may hold values from -6 to 6
- saved_x: bfloat16 [2, 16, 256, 7168], P(None, 'section', 'expert'), may hold values from -6 to 6
- saved_gate: bfloat16 [2, 16, 256, 4096], P(None, 'section', None, 'expert'), may hold values from -8 to 8
- saved_up: bfloat16 [2, 16, 256, 4096], P(None, 'section', None, 'expert'), may hold values from -6 to 6
- fwd_order: int32 [2, 16, 256, 2], P(None, 'section'), may hold values from 0 to 1, each once within a row
- fwd_weight: float32 [2, 16, 256, 2], P(None, 'section'), may hold values from 0.25 to 2
- bwd_order: int32 [2, 16, 256, 2], P(None, 'section'), may hold values from 0 to 1, each once within a row
- bwd_weight: float32 [2, 16, 256, 2], P(None, 'section'), may hold values from 0.25 to 2
- w_gate: bfloat16 [16, 7168, 4096], P('section', None, 'expert'), may hold values from -0.0625 to 0.0625
- w_up: bfloat16 [16, 7168, 4096], P('section', None, 'expert'), may hold values from -0.0625 to 0.0625
- w_down: bfloat16 [16, 4096, 7168], P('section', 'expert'), may hold values from -0.125 to 0.125
Outputs:
- fwd_out: bfloat16 [16, 256, 7168], P('section', 'expert')
- bwd_out: bfloat16 [16, 256, 7168], P('section', 'expert')
The draws below stay inside these ranges and needn't reach their ends.
Inputs may be any that keep to these rules, and one draw needn't show every extreme that they name: `fwd_order`: each token's row names every expert of the window exactly once. `bwd_order`: each token's row names every expert of the window exactly once.
All inputs are finite; a program needn't handle non-finite values.
Results may differ from the reference program's by a relative error of at most 0.033.
Values may be sent and summed in bfloat16 or wider, within the bound.
No kernel may reach another device: no remote copies, remote signals or barrier semaphores. Data moves between devices by JAX's collectives and lax.ppermute only.
A program may use at most 128 MiB of HBM per device.

```python
import math
import jax
import jax.numpy as jnp
from jax import lax

D = 7168
FF = 2048
EXPERTS = 2
TOK = 256
UNITS = 4096
SECTIONS = 16
N_EXPERT = 16


def level_of(stream_key, extent, pieces, least, high):
    factor_of, own = 1.0, jax.random.fold_in(stream_key, 6)
    for axis_at, blocks in pieces:
        steps = jnp.exp(jax.random.uniform(jax.random.fold_in(own, axis_at), (blocks,), jnp.float32, least / len(pieces), high / len(pieces)))
        factor_of = factor_of * jnp.repeat(steps, extent[axis_at] // blocks).reshape([-1 if axis == axis_at else 1 for axis in range(len(extent))])
    return factor_of


def noise(own_key, extent, scale, most, split=(), kind=jnp.bfloat16):
    entries = scale * jax.random.normal(own_key, extent, jnp.float32)
    if split:
        entries = entries * level_of(own_key, extent, split, -0.22, 0.18)
    return jnp.clip(entries, -most, most).astype(kind)


def setup_inputs(seed: int = 0) -> dict:
    seeds = jax.random.split(jax.random.key(seed), 15)
    return {
        "fwd_in": noise(seeds[0], (SECTIONS, TOK, D), 1.0, 6.0, ((0, 16), (1, 16))),
        "fwd_new": noise(seeds[1], (TOK, D), 1.0, 6.0, ((0, 16),)),
        "grad_in": noise(seeds[2], (SECTIONS, TOK, D), 1.0, 6.0, ((0, 16), (1, 16))),
        "grad_new": noise(seeds[3], (TOK, D), 1.0, 6.0, ((0, 16),)),
        "saved_x": noise(seeds[4], (2, SECTIONS, TOK, D), 1.0, 6.0, ((1, 16), (2, 16))),
        "saved_gate": noise(seeds[5], (2, SECTIONS, TOK, UNITS), 1.5, 8.0, ((1, 16), (3, 16))),
        "saved_up": noise(seeds[6], (2, SECTIONS, TOK, UNITS), 1.0, 6.0, ((1, 16), (3, 16))),
        "fwd_order": jax.vmap(lambda own: jax.random.permutation(own, EXPERTS))(jax.random.split(seeds[7], 2 * SECTIONS * TOK)).reshape((2, SECTIONS, TOK, EXPERTS)).astype(jnp.int32),
        "fwd_weight": jnp.clip(jnp.exp(math.log(2.0) - 2.0794415 * jax.random.uniform(seeds[8], (2, SECTIONS, TOK, EXPERTS), jnp.float32) ** level_of(seeds[8], (2, SECTIONS, TOK, EXPERTS), ((1, 16),), -0.2, 0.2)), 0.25, 2.0),
        "bwd_order": jax.vmap(lambda own: jax.random.permutation(own, EXPERTS))(jax.random.split(seeds[9], 2 * SECTIONS * TOK)).reshape((2, SECTIONS, TOK, EXPERTS)).astype(jnp.int32),
        "bwd_weight": jnp.clip(jnp.exp(math.log(2.0) - 2.0794415 * jax.random.uniform(seeds[10], (2, SECTIONS, TOK, EXPERTS), jnp.float32) ** level_of(seeds[10], (2, SECTIONS, TOK, EXPERTS), ((1, 16),), -0.2, 0.2)), 0.25, 2.0),
        "w_gate": noise(seeds[11], (SECTIONS, D, UNITS), D ** -0.5, 0.0625, ((0, 16), (2, 16))),
        "w_up": noise(seeds[12], (SECTIONS, D, UNITS), D ** -0.5, 0.0625, ((0, 16), (2, 16))),
        "w_down": noise(seeds[13], (SECTIONS, UNITS, D), FF ** -0.5, 0.125, ((0, 16), (1, 16))),
    }


EPS = 1e-06

def normalize(v):
    v = v.astype(jnp.float32)
    return v * lax.rsqrt(lax.optimization_barrier(jnp.mean(v * v, axis=-1, keepdims=True)) + EPS)

def normal_back(x, cot):
    _, pull = jax.vjp(normalize, x.astype(jnp.float32))
    return pull(cot)[0]

def route_scale(order, weight):
    count = weight.shape[-1]
    hits = (order[..., None] == jnp.arange(count, dtype=jnp.int32)).astype(jnp.float32)
    per_expert = lax.optimization_barrier(jnp.sum(hits * weight[..., None, :], axis=-1))
    return jnp.repeat(per_expert, FF, axis=1)

def rounded(term):
    return lax.optimization_barrier(term.astype(jnp.bfloat16)).astype(jnp.float32)

def layer_forward(args):
    x, order, weight, w_gate, w_up, w_down = args
    tokens = x.shape[0]
    block = w_gate.shape[1] // N_EXPERT
    xn = normalize(x).astype(jnp.bfloat16)
    gate = jnp.dot(xn, w_gate, preferred_element_type=jnp.float32)
    up = jnp.dot(xn, w_up, preferred_element_type=jnp.float32)
    scale = route_scale(order, weight)
    hidden = (scale * jax.nn.silu(gate) * up).astype(jnp.bfloat16)
    left = hidden.reshape(tokens, N_EXPERT, block).transpose(1, 0, 2)
    right = w_down.reshape(N_EXPERT, block, -1)

    def step(carry, pair):
        term = jnp.dot(pair[0], pair[1], preferred_element_type=jnp.float32)
        return (carry + rounded(term), None)
    branch, _ = lax.scan(step, jnp.zeros((tokens, x.shape[1]), jnp.float32), (left, right))
    return (x.astype(jnp.float32) + branch).astype(jnp.bfloat16)

def layer_backward(args):
    g, x, s_gate, s_up, order, weight, w_gate, w_up, w_down = args
    tokens = g.shape[0]
    width = g.shape[1]
    block = w_gate.shape[1] // N_EXPERT
    dh = jnp.dot(g, w_down.T, preferred_element_type=jnp.float32)
    scale = route_scale(order, weight)
    sg = s_gate.astype(jnp.float32)
    sig = jax.nn.sigmoid(sg)
    dgate = (dh * scale * s_up.astype(jnp.float32) * (sig * (1.0 + sg * (1.0 - sig)))).astype(jnp.bfloat16)
    dup = (dh * scale * (sg * sig)).astype(jnp.bfloat16)
    left_g = dgate.reshape(tokens, N_EXPERT, block).transpose(1, 0, 2)
    left_u = dup.reshape(tokens, N_EXPERT, block).transpose(1, 0, 2)
    right_g = w_gate.reshape(width, N_EXPERT, block).transpose(1, 2, 0)
    right_u = w_up.reshape(width, N_EXPERT, block).transpose(1, 2, 0)

    def step(carry, parts):
        term = jnp.dot(parts[0], parts[2], preferred_element_type=jnp.float32)
        term = term + jnp.dot(parts[1], parts[3], preferred_element_type=jnp.float32)
        return (carry + rounded(term), None)
    dxn, _ = lax.scan(step, jnp.zeros((tokens, width), jnp.float32), (left_g, left_u, right_g, right_u))
    return (g.astype(jnp.float32) + normal_back(x, dxn)).astype(jnp.bfloat16)

def reference(fwd_in, fwd_new, grad_in, grad_new, saved_x, saved_gate, saved_up, fwd_order, fwd_weight, bwd_order, bwd_weight, w_gate, w_up, w_down):
    first_out = lax.map(layer_forward, (fwd_in, fwd_order[0], fwd_weight[0], w_gate, w_up, w_down))
    first_grad = lax.map(layer_backward, (grad_in, saved_x[0], saved_gate[0], saved_up[0], bwd_order[0], bwd_weight[0], w_gate, w_up, w_down))
    second_in = jnp.concatenate([fwd_new[None], first_out[:-1]], axis=0)
    second_grad = jnp.concatenate([first_grad[1:], grad_new[None]], axis=0)
    fwd_out = lax.map(layer_forward, (second_in, fwd_order[1], fwd_weight[1], w_gate, w_up, w_down))
    bwd_out = lax.map(layer_backward, (second_grad, saved_x[1], saved_gate[1], saved_up[1], bwd_order[1], bwd_weight[1], w_gate, w_up, w_down))
    return (fwd_out, bwd_out)
```

```python
import jax
import jax.numpy as jnp
from jax import lax
from jax.sharding import PartitionSpec as P

FF = 2048
EPS = 1e-06
BF16 = jnp.bfloat16
F32 = jnp.float32

NY, NX, NC = 4, 2, 2
ROWS = 16


def perm(dy, dx, dc):
    def at(y, x, c):
        return ((y % NY) * NX + x % NX) * NC + c % NC

    return [(at(y, x, c), at(y + dy, x + dx, c + dc)) for y in range(NY) for x in range(NX) for c in range(NC)]


def send(value, dy, dx=0, dc=0):
    return lax.ppermute(value, "expert", perm(dy, dx, dc))


def from_behind(value, axis, steps):
    count = lax.axis_size(axis)
    initial, last = (max(0, -steps), min(count, count - steps))
    return lax.ppermute(value, axis, [(source, source + steps) for source in range(initial, last)])


def gather(own):
    xp = send(own, 0, 1)
    yp = send(own, -1)
    ym = send(own, 1)
    y2 = send(own, 2)
    xyp = send(xp, -1)
    xym = send(xp, 1)
    xy2 = send(y2, 0, 1)
    return jnp.concatenate([own, xp, yp, xyp, y2, xy2, ym, xym], axis=0)


def total(*parts):
    result = parts[0].astype(F32)
    for part in parts[1:]:
        result = result + part.astype(F32)
    return result


def reduce(partial):
    own, xp, yp, xyp, y2, xy2, ym, xym = (partial[ROWS * k : ROWS * (k + 1)] for k in range(8))
    from_yp = send(xyp, 1)
    from_ym = send(xym, -1)
    from_x = send(xy2, 0, 1)
    a = send(yp, 1)
    b = send(ym, -1)
    c = send(total(xp, from_yp, from_ym).astype(BF16), 0, 1)
    d = send(total(y2, from_x).astype(BF16), 2)
    return total(own, a, b, c, d)


def normalize(v):
    v = v.astype(F32)
    return v * lax.rsqrt(jnp.mean(v * v, axis=-1, keepdims=True) + EPS)


def normal_back(x, cot):
    _, pull = jax.vjp(normalize, x.astype(F32))
    return pull(cot)[0]


def dot(a, b):
    return jnp.dot(a, b, preferred_element_type=F32)


def dot_t(a, b):
    return lax.dot_general(a, b, (((1,), (1,)), ((), ())), preferred_element_type=F32)


def local(
    fwd_in,
    fwd_new,
    grad_in,
    grad_new,
    saved_x,
    saved_gate,
    saved_up,
    fwd_order,
    fwd_weight,
    bwd_order,
    bwd_weight,
    w_gate,
    w_up,
    w_down,
):
    columns = w_gate.shape[2]
    index = lax.axis_index("expert")
    y, x, core = index // (NX * NC), index // NC % NX, index % NC
    owner = index * columns // FF
    section_now = lax.axis_index("section")
    is_first = section_now == 0
    is_last = section_now == lax.axis_size("section") - 1

    def by_place(value):
        lead, tail = value.shape[0], value.shape[2:]
        value = value.reshape((lead, NY, NX, NC, ROWS) + tail)
        value = lax.dynamic_slice_in_dim(jnp.concatenate([value, value], axis=1), y, NY, axis=1)
        value = jnp.where(x == 0, value, value[:, :, ::-1])
        first, second = (value[:, :, :, k].reshape((lead, NY * NX * ROWS) + tail) for k in range(NC))
        return jnp.where(core == 0, first, second), jnp.where(core == 0, second, first)

    def route_scale(order, weight):
        count = weight.shape[-1]
        hits = (order[..., None] == jnp.arange(count, dtype=jnp.int32)).astype(F32)
        per_expert = jnp.sum(hits * weight[..., None, :], axis=-1)
        pick = (jnp.arange(count, dtype=jnp.int32) == owner).astype(F32)
        return by_place(jnp.sum(per_expert * pick, axis=-1))[0]

    gates = [w_gate[0], send(w_gate[0], 0, 0, 1)]
    ups = [w_up[0], send(w_up[0], 0, 0, 1)]
    downs = [w_down[0], send(w_down[0], 0, 0, 1)]
    gates_t = [w.T for w in gates]
    ups_t = [w.T for w in ups]

    fwd_scale = route_scale(fwd_order[:, 0], fwd_weight[:, 0])
    bwd_scale = route_scale(bwd_order[:, 0], bwd_weight[:, 0])
    mine, others = by_place(jnp.concatenate([saved_gate[:, 0], saved_up[:, 0]], axis=0))
    theirs = send(others, 0, 0, 1)
    saved = [mine, theirs]

    def forward(rows, which):
        scale = fwd_scale[which][:, None]
        full = gather(normalize(rows).astype(BF16))
        partial = 0.0
        for gate_w, up_w, down_w in zip(gates, ups, downs):
            hidden = (scale * jax.nn.silu(dot(full, gate_w)) * dot(full, up_w)).astype(BF16)
            partial = partial + dot(hidden, down_w)
        return (rows.astype(F32) + reduce(partial.astype(BF16))).astype(BF16)

    def backward(rows, which):
        scale = bwd_scale[which][:, None]
        full = gather(rows)
        partial = 0.0
        for gate_t, up_t, down_w, pair in zip(gates_t, ups_t, downs, saved):
            dh = dot_t(full, down_w) * scale
            sg, su = pair[which].astype(F32), pair[2 + which].astype(F32)
            sig = jax.nn.sigmoid(sg)
            dgate = (dh * su * (sig * (1.0 + sg * (1.0 - sig)))).astype(BF16)
            dup = (dh * (sg * sig)).astype(BF16)
            partial = partial + dot(dgate, gate_t) + dot(dup, up_t)
        dxn = reduce(partial.astype(BF16))
        return (rows.astype(F32) + normal_back(saved_x[which, 0], dxn)).astype(BF16)

    first_out = forward(fwd_in[0], 0)
    first_grad = backward(grad_in[0], 0)
    second_in = jnp.where(is_first, fwd_new, from_behind(first_out, "section", 1))
    second_grad = jnp.where(is_last, grad_new, from_behind(first_grad, "section", -1))
    return (forward(second_in, 1)[None], backward(second_grad, 1)[None])


def solution(mesh):
    return jax.shard_map(
        local,
        mesh=mesh,
        in_specs=(
            P("section", "expert", None),
            P("expert", None),
            P("section", "expert", None),
            P("expert", None),
            P(None, "section", "expert", None),
            P(None, "section", None, "expert"),
            P(None, "section", None, "expert"),
            P(None, "section", None, None),
            P(None, "section", None, None),
            P(None, "section", None, None),
            P(None, "section", None, None),
            P("section", None, "expert"),
            P("section", None, "expert"),
            P("section", "expert", None),
        ),
        out_specs=(P("section", "expert", None), P("section", "expert", None)),
        check_vma=False,
    )
```

```python
import functools

import jax
import jax.numpy as jnp
from jax import lax
from jax.experimental import pallas as pl
from jax.experimental.pallas import tpu as pltpu
from jax.sharding import PartitionSpec as P

FF = 2048
EPS = 1e-06
BF16 = jnp.bfloat16
F32 = jnp.float32

NY, NX, NC = 4, 2, 2
ROWS = 16
TILE = 1024

PIECES = ((0, 1), (1, 1), (2, 2), (4, 1), (5, 1), (6, 2))

ANY = pl.BlockSpec(memory_space=pl.ANY)
VMEM = pl.BlockSpec(memory_space=pltpu.VMEM)


def perm(dy, dx, dc):
    def at(y, x, c):
        return ((y % NY) * NX + x % NX) * NC + c % NC

    return [(at(y, x, c), at(y + dy, x + dx, c + dc)) for y in range(NY) for x in range(NX) for c in range(NC)]


def send(value, dy, dx=0, dc=0):
    return lax.ppermute(value, "expert", perm(dy, dx, dc))


def from_behind(value, axis, steps):
    count = lax.axis_size(axis)
    initial, last = (max(0, -steps), min(count, count - steps))
    return lax.ppermute(value, axis, [(source, source + steps) for source in range(initial, last)])


def dot(a, b):
    return jnp.dot(a, b, preferred_element_type=F32)


def dot_t(a, b):
    return lax.dot_general(a, b, (((1,), (1,)), ((), ())), preferred_element_type=F32)


def rows_of(piece):
    return slice(ROWS * piece[0], ROWS * (piece[0] + piece[1]))


def forward_kernel(tokens, *refs):
    shards, scale, gates, ups, downs = refs[:6], refs[6], refs[7:9], refs[9:11], refs[11:13]
    outs, (full, hidden) = refs[13 + tokens : 19 + tokens], refs[19 + tokens :]
    for shard, piece in zip(shards, PIECES):
        full[rows_of(piece), :] = shard[...]
    units = gates[0].shape[1]
    for i in range(2):
        gate = dot(full[...], gates[i][...])
        up = dot(full[...], ups[i][...])
        hidden[:, units * i : units * (i + 1)] = (scale[...] * (gate * jax.nn.sigmoid(gate)) * up).astype(BF16)
    for start in range(0, full.shape[1], TILE):
        cols = slice(start, start + TILE)
        part = dot(hidden[:, :units], downs[0][:, cols]) + dot(hidden[:, units:], downs[1][:, cols])
        part = part.astype(BF16)
        for out, piece in zip(outs, PIECES):
            out[:, cols] = part[rows_of(piece)]


def backward_kernel(tokens, *refs):
    shards, scale, saved, gates, ups, downs = refs[:6], refs[6], refs[7:11], refs[11:13], refs[13:15], refs[15:17]
    outs, (full, inner) = refs[17 + tokens : 23 + tokens], refs[23 + tokens :]
    for shard, piece in zip(shards, PIECES):
        full[rows_of(piece), :] = shard[...]
    units = gates[0].shape[1]
    for i in range(2):
        dh = dot_t(full[...], downs[i][...]) * scale[...]
        sg, su = saved[2 * i][...].astype(F32), saved[2 * i + 1][...].astype(F32)
        sig = jax.nn.sigmoid(sg)
        inner[2 * i] = (dh * su * (sig * (1.0 + sg * (1.0 - sig)))).astype(BF16)
        inner[2 * i + 1] = (dh * (sg * sig)).astype(BF16)
    weights = (gates[0], ups[0], gates[1], ups[1])
    for start in range(0, full.shape[1], TILE):
        cols = slice(start, start + TILE)
        part = dot(inner[0], weights[0][:, cols])
        for i in range(1, 4):
            part = part + dot(inner[i], weights[i][:, cols])
        part = part.astype(BF16)
        for out, piece in zip(outs, PIECES):
            out[:, cols] = part[rows_of(piece)]


def in_vmem(value):
    return pltpu.with_memory_space_constraint(value, pltpu.VMEM)


def in_hbm(value):
    return pltpu.with_memory_space_constraint(value, pltpu.HBM)


def hold_kernel(gate, up, down, *refs):
    gate_out, gate_t, up_out, up_t, down_out, sems = refs[-6:]
    pairs = ((gate, gate_out), (up, up_out), (down, down_out))
    copies = [pltpu.make_async_copy(a, b, sems.at[i]) for i, (a, b) in enumerate(pairs)]
    for copy in copies:
        copy.start()
    for copy, whole, turned in ((copies[0], gate_out, gate_t), (copies[1], up_out, up_t)):
        copy.wait()
        for start in range(0, whole.shape[0], TILE):
            turned[:, start : start + TILE] = whole[start : start + TILE, :].T
    copies[2].wait()


def hold(gate, up, down, tokens):
    width, units = gate.shape
    tall, flat = pltpu.VMEM((width, units), BF16), pltpu.VMEM((units, width), BF16)
    return pl.pallas_call(
        hold_kernel,
        out_shape=[tall, flat, tall, flat, flat],
        in_specs=[ANY] * (3 + len(tokens)),
        out_specs=[VMEM] * 5,
        scratch_shapes=[pltpu.SemaphoreType.DMA((3,))],
        compiler_params=pltpu.CompilerParams(vmem_limit_bytes=2 << 20),
        cost_estimate=pl.CostEstimate(flops=0, bytes_accessed=6 * width * units, transcendentals=0),
        name="hold",
    )(in_hbm(gate), in_hbm(up), in_hbm(down), *tokens)


def layer(kernel, name, shards, small, weights, scratch, tokens):
    width = weights[-1].shape[1]
    count = ROWS * NY * NX
    units = weights[-1].shape[0]
    operands = [*map(in_vmem, shards), *small, *map(in_vmem, weights)]
    return pl.pallas_call(
        functools.partial(kernel, len(tokens)),
        out_shape=[OUT(ROWS * blocks, width) for _, blocks in PIECES],
        in_specs=[VMEM] * len(operands) + [ANY] * len(tokens),
        out_specs=[VMEM] * 6,
        scratch_shapes=[pltpu.VMEM((count, width), BF16), scratch],
        compiler_params=pltpu.CompilerParams(vmem_limit_bytes=8 << 20),
        cost_estimate=pl.CostEstimate(
            flops=12 * count * units * width, bytes_accessed=4 * count * width, transcendentals=2 * count * units
        ),
        name=name,
    )(*operands, *tokens)


def pair_kernel(tokens, first, second, *refs):
    out, sems = refs[tokens:]
    copies = [
        pltpu.make_async_copy(first, out.at[pl.ds(0, ROWS)], sems.at[0]),
        pltpu.make_async_copy(second, out.at[pl.ds(ROWS, ROWS)], sems.at[1]),
    ]
    for copy in copies:
        copy.start()
    for copy in copies:
        copy.wait()


def pair(first, second, tokens):
    return pl.pallas_call(
        functools.partial(pair_kernel, len(tokens)),
        out_shape=OUT(2 * ROWS, first.shape[1]),
        in_specs=[ANY] * (2 + len(tokens)),
        out_specs=ANY,
        scratch_shapes=[pltpu.SemaphoreType.DMA((2,))],
        compiler_params=pltpu.CompilerParams(vmem_limit_bytes=1 << 20),
        name="pair",
    )(first, second, *tokens)


def tie_kernel(*refs):
    pass


def tie(value, tokens):
    return pl.pallas_call(
        tie_kernel,
        out_shape=jax.ShapeDtypeStruct(value.shape, value.dtype),
        in_specs=[ANY] * (1 + len(tokens)),
        out_specs=ANY,
        input_output_aliases={0: 0},
        compiler_params=pltpu.CompilerParams(vmem_limit_bytes=1 << 20),
        name="tie",
    )(value, *tokens)


def OUT(rows, width):
    return pltpu.VMEM((rows, width), BF16)


def gather_near(own):
    return send(own, 0, 1), send(own, 2)


def gather_far(own, near, tokens):
    xp, y2 = near
    both = pair(own, xp, tokens)
    return own, xp, send(both, -1), y2, send(y2, 0, 1), send(both, 1)


def total(*parts):
    result = parts[0].astype(F32)
    for part in parts[1:]:
        result = result + part.astype(F32)
    return result


def reduce_far(pieces):
    return send(pieces[2], 1), send(pieces[5], -1), send(pieces[4], 0, 1)


def reduce_near(pieces, far):
    from_yp, from_ym, from_x = far
    to_x = total(pieces[1], from_yp[ROWS:], from_ym[ROWS:]).astype(BF16)
    to_y2 = total(pieces[3], from_x).astype(BF16)
    return (to_x, to_y2), (send(to_x, 0, 1), send(to_y2, 2))


def reduce_end(pieces, far, near):
    return total(pieces[0], far[0][:ROWS], far[1][:ROWS], near[0], near[1])


def normalize(v):
    v = v.astype(F32)
    return v * lax.rsqrt(jnp.mean(v * v, axis=-1, keepdims=True) + EPS)


def normal_back(x, cot):
    _, pull = jax.vjp(normalize, x.astype(F32))
    return pull(cot)[0]


def local(
    fwd_in,
    fwd_new,
    grad_in,
    grad_new,
    saved_x,
    saved_gate,
    saved_up,
    fwd_order,
    fwd_weight,
    bwd_order,
    bwd_weight,
    w_gate,
    w_up,
    w_down,
):
    columns = w_gate.shape[2]
    index = lax.axis_index("expert")
    y, x, core = index // (NX * NC), index // NC % NX, index % NC
    owner = index * columns // FF
    section_now = lax.axis_index("section")
    is_first = section_now == 0
    is_last = section_now == lax.axis_size("section") - 1

    def by_place(value):
        lead, tail = value.shape[0], value.shape[2:]
        value = value.reshape((lead, NY, NX, NC, ROWS) + tail)
        value = lax.dynamic_slice_in_dim(jnp.concatenate([value, value], axis=1), y, NY, axis=1)
        value = jnp.where(x == 0, value, value[:, :, ::-1])
        first, second = (value[:, :, :, k].reshape((lead, NY * NX * ROWS) + tail) for k in range(NC))
        return jnp.where(core == 0, first, second), jnp.where(core == 0, second, first)

    def route_scale(order, weight):
        count = weight.shape[-1]
        hits = (order[..., None] == jnp.arange(count, dtype=jnp.int32)).astype(F32)
        per_expert = jnp.sum(hits * weight[..., None, :], axis=-1)
        pick = (jnp.arange(count, dtype=jnp.int32) == owner).astype(F32)
        return by_place(jnp.sum(per_expert * pick, axis=-1))[0]

    fwd_scale = [route_scale(fwd_order[k : k + 1, 0], fwd_weight[k : k + 1, 0]).reshape(-1, 1) for k in range(2)]
    bwd_scale = [route_scale(bwd_order[k : k + 1, 0], bwd_weight[k : k + 1, 0]).reshape(-1, 1) for k in range(2)]
    mine, others = by_place(jnp.concatenate([saved_gate[:, 0], saved_up[:, 0]], axis=0))
    theirs = send(others, 0, 0, 1)
    mine = [mine[k] for k in range(4)]
    new_rows = jnp.where(is_first, fwd_new, jnp.zeros_like(fwd_new))
    new_grads = jnp.where(is_last, grad_new, jnp.zeros_like(grad_new))

    early = [*fwd_scale, *bwd_scale, *mine, new_rows, new_grads]
    weights = [w_gate[0], w_up[0], w_down[0]]
    x_first = normalize(fwd_in[0]).astype(BF16)
    own = hold(*weights, (x_first, *early))
    x_first_near = gather_near(x_first)
    peer = hold(*[send(w, 0, 0, 1) for w in weights], x_first_near)
    gates, gates_t, ups, ups_t, downs = map(list, zip(own, peer))


    def forward(shards, which, tokens=()):
        return layer(
            forward_kernel,
            "forward",
            shards,
            [fwd_scale[which]],
            [*gates, *ups, *downs],
            pltpu.VMEM((ROWS * NY * NX, 2 * columns), BF16),
            tokens,
        )

    def backward(shards, which, tokens=()):
        saved = [mine[which], mine[2 + which], theirs[which], theirs[2 + which]]
        return layer(
            backward_kernel,
            "backward",
            shards,
            [bwd_scale[which], *saved],
            [*gates_t, *ups_t, *downs],
            pltpu.VMEM((4, ROWS * NY * NX, columns), BF16),
            tokens,
        )

    def tick(x_rows, g_rows, which, xn, x_near):
        x_shards = gather_far(xn, x_near, ())
        g_rows = tie(g_rows, x_near)
        g_near = gather_near(g_rows)
        x_parts = forward(x_shards, which)
        x_far = reduce_far(x_parts)
        g_shards = gather_far(g_rows, g_near, x_parts[:1])
        x_sent, x_close = reduce_near(x_parts, x_far)
        g_parts = backward(g_shards, which, x_sent)
        g_far = reduce_far(g_parts)
        x_out = (x_rows.astype(F32) + reduce_end(x_parts, x_far, x_close)).astype(BF16)
        _, g_close = reduce_near(g_parts, g_far)
        dxn = reduce_end(g_parts, g_far, g_close)
        g_out = (g_rows.astype(F32) + normal_back(saved_x[which, 0], dxn)).astype(BF16)
        return x_out, g_out

    first_out, first_grad = tick(fwd_in[0], grad_in[0], 0, x_first, x_first_near)
    second_in = from_behind(first_out, "section", 1) + new_rows
    second_grad = from_behind(first_grad, "section", -1) + new_grads
    x_second = normalize(second_in).astype(BF16)
    final_out, final_grad = tick(second_in, second_grad, 1, x_second, gather_near(x_second))
    return (final_out[None], final_grad[None])


def solution(mesh):
    return jax.shard_map(
        local,
        mesh=mesh,
        in_specs=(
            P("section", "expert", None),
            P("expert", None),
            P("section", "expert", None),
            P("expert", None),
            P(None, "section", "expert", None),
            P(None, "section", None, "expert"),
            P(None, "section", None, "expert"),
            P(None, "section", None, None),
            P(None, "section", None, None),
            P(None, "section", None, None),
            P(None, "section", None, None),
            P("section", None, "expert"),
            P("section", None, "expert"),
            P("section", "expert", None),
        ),
        out_specs=(P("section", "expert", None), P("section", "expert", None)),
        check_vma=False,
    )
```

```python
import functools

import jax
import jax.numpy as jnp
from jax import lax
from jax.experimental import pallas as pl
from jax.experimental.pallas import tpu as pltpu
from jax.sharding import PartitionSpec as P

FF = 2048
EPS = 1e-06
BF16 = jnp.bfloat16
F32 = jnp.float32

NY, NX, NC = 4, 2, 2
ROWS = 16
TILE = 1024

PIECES = ((0, 1), (1, 1), (2, 2), (4, 1), (5, 1), (6, 2))

SMALL = pl.CostEstimate(flops=0, bytes_accessed=0, transcendentals=0)

ANY = pl.BlockSpec(memory_space=pl.ANY)
VMEM = pl.BlockSpec(memory_space=pltpu.VMEM)


def perm(dy, dx, dc):
    def at(y, x, c):
        return ((y % NY) * NX + x % NX) * NC + c % NC

    return [(at(y, x, c), at(y + dy, x + dx, c + dc)) for y in range(NY) for x in range(NX) for c in range(NC)]


def send(value, dy, dx=0, dc=0):
    return lax.ppermute(value, "expert", perm(dy, dx, dc))


def from_behind(value, axis, steps):
    count = lax.axis_size(axis)
    initial, last = (max(0, -steps), min(count, count - steps))
    return lax.ppermute(value, axis, [(source, source + steps) for source in range(initial, last)])


def dot(a, b):
    return jnp.dot(a, b, preferred_element_type=F32)


def dot_t(a, b):
    return lax.dot_general(a, b, (((1,), (1,)), ((), ())), preferred_element_type=F32)


def rows_of(piece):
    return slice(ROWS * piece[0], ROWS * (piece[0] + piece[1]))


def fill(full, shards, first):
    for shard, (block, blocks) in zip(shards, PIECES):
        stride = shard.shape[0] // (ROWS * blocks)
        for k in range(blocks):
            start = ROWS * (stride * k + first)
            full[ROWS * (block + k) : ROWS * (block + k + 1), :] = shard[start : start + ROWS, :]


def forward_kernel(tokens, first, *refs):
    shards, scale, gates, ups, downs = refs[:6], refs[6], refs[7:9], refs[9:11], refs[11:13]
    outs, (full, hidden) = refs[13 + tokens : 19 + tokens], refs[19 + tokens :]
    fill(full, shards, first)
    units = gates[0].shape[1]
    for i in range(2):
        gate = dot(full[...], gates[i][...])
        up = dot(full[...], ups[i][...])
        hidden[:, units * i : units * (i + 1)] = (scale[...] * (gate * jax.nn.sigmoid(gate)) * up).astype(BF16)
    for start in range(0, full.shape[1], TILE):
        cols = slice(start, start + TILE)
        part = dot(hidden[:, :units], downs[0][:, cols]) + dot(hidden[:, units:], downs[1][:, cols])
        part = part.astype(BF16)
        for out, piece in zip(outs, PIECES):
            out[:, cols] = part[rows_of(piece)]


def backward_kernel(tokens, first, *refs):
    shards, scale, saved, gates, ups, downs = refs[:6], refs[6], refs[7:11], refs[11:13], refs[13:15], refs[15:17]
    outs, (full, inner) = refs[17 + tokens : 23 + tokens], refs[23 + tokens :]
    fill(full, shards, first)
    units = gates[0].shape[1]
    for i in range(2):
        dh = dot_t(full[...], downs[i][...]) * scale[...]
        sg, su = saved[2 * i][...].astype(F32), saved[2 * i + 1][...].astype(F32)
        sig = jax.nn.sigmoid(sg)
        inner[2 * i] = (dh * su * (sig * (1.0 + sg * (1.0 - sig)))).astype(BF16)
        inner[2 * i + 1] = (dh * (sg * sig)).astype(BF16)
    weights = (gates[0], ups[0], gates[1], ups[1])
    for start in range(0, full.shape[1], TILE):
        cols = slice(start, start + TILE)
        part = dot(inner[0], weights[0][:, cols])
        for i in range(1, 4):
            part = part + dot(inner[i], weights[i][:, cols])
        part = part.astype(BF16)
        for out, piece in zip(outs, PIECES):
            out[:, cols] = part[rows_of(piece)]


def OUT(rows, width):
    return pltpu.VMEM((rows, width), BF16)


def in_vmem(value):
    return pltpu.with_memory_space_constraint(value, pltpu.VMEM)


def in_hbm(value):
    return pltpu.with_memory_space_constraint(value, pltpu.HBM)


def hold_kernel(gate, up, down, *refs):
    gate_out, gate_t, up_out, up_t, down_out, sems = refs[-6:]
    pairs = ((gate, gate_out), (up, up_out), (down, down_out))
    copies = [pltpu.make_async_copy(a, b, sems.at[i]) for i, (a, b) in enumerate(pairs)]
    for copy in copies:
        copy.start()
    for copy, whole, turned in ((copies[0], gate_out, gate_t), (copies[1], up_out, up_t)):
        copy.wait()
        for start in range(0, whole.shape[0], TILE):
            turned[:, start : start + TILE] = whole[start : start + TILE, :].T
    copies[2].wait()


def hold(gate, up, down, tokens):
    width, units = gate.shape
    tall, flat = pltpu.VMEM((width, units), BF16), pltpu.VMEM((units, width), BF16)
    return pl.pallas_call(
        hold_kernel,
        out_shape=[tall, flat, tall, flat, flat],
        in_specs=[ANY] * (3 + len(tokens)),
        out_specs=[VMEM] * 5,
        scratch_shapes=[pltpu.SemaphoreType.DMA((3,))],
        compiler_params=pltpu.CompilerParams(vmem_limit_bytes=2 << 20),
        cost_estimate=SMALL,
        name="hold",
    )(in_hbm(gate), in_hbm(up), in_hbm(down), *tokens)


def layer(kernel, name, shards, first, small, weights, scratch, tokens):
    width = weights[-1].shape[1]
    count = ROWS * NY * NX
    units = weights[-1].shape[0]
    operands = [*map(in_vmem, shards), *small, *map(in_vmem, weights)]
    return pl.pallas_call(
        functools.partial(kernel, len(tokens), first),
        out_shape=[OUT(ROWS * blocks, width) for _, blocks in PIECES],
        in_specs=[VMEM] * len(operands) + [ANY] * len(tokens),
        out_specs=[VMEM] * 6,
        scratch_shapes=[pltpu.VMEM((count, width), BF16), scratch],
        compiler_params=pltpu.CompilerParams(vmem_limit_bytes=4 << 20),
        cost_estimate=SMALL,
        name=name,
    )(*operands, *tokens)


def prepare_kernel(
    tokens, place, fwd_order, fwd_weight, bwd_order, bwd_weight, saved_gate, saved_up, fwd_new, grad_new, *refs
):
    outs = refs[tokens:]
    scales, mine, others = outs[:4], outs[4:8], outs[8]
    outs[9][...] = jnp.where(place[4] == 1, fwd_new[...], jnp.zeros_like(fwd_new))
    outs[10][...] = jnp.where(place[5] == 1, grad_new[...], jnp.zeros_like(grad_new))
    y, x, core, owner = (place[i] for i in range(4))
    for k in range(NY * NX):
        chip = lax.rem(y + k // NX, NY) * NX + lax.rem(x + k % NX, NX)
        rows = slice(ROWS * k, ROWS * (k + 1))
        here = pl.ds(pl.multiple_of((chip * NC + core) * ROWS, ROWS), ROWS)
        there = pl.ds(pl.multiple_of((chip * NC + 1 - core) * ROWS, ROWS), ROWS)
        for which in range(2):
            for i, (order, weight) in enumerate(((fwd_order, fwd_weight), (bwd_order, bwd_weight))):
                o, w = order[which, here, :], weight[which, here, :]
                column = jnp.where(owner == 0, o[:, :1], o[:, 1:])
                scales[2 * i + which][rows, :] = jnp.where(column == 0, w[:, :1], w[:, 1:])
            for i, saved in enumerate((saved_gate, saved_up)):
                mine[2 * i + which][rows, :] = saved[which, here, :]
                others[2 * i + which, rows, :] = saved[which, there, :]


def prepare(place, routes, saved, new, tokens):
    count, units = ROWS * NY * NX, saved[0].shape[2]
    return pl.pallas_call(
        functools.partial(prepare_kernel, len(tokens)),
        out_shape=[jax.ShapeDtypeStruct((count, 1), F32)] * 4
        + [jax.ShapeDtypeStruct((count, units), BF16)] * 4
        + [jax.ShapeDtypeStruct((4, count, units), BF16)]
        + [jax.ShapeDtypeStruct(v.shape, BF16) for v in new],
        in_specs=[pl.BlockSpec(memory_space=pltpu.SMEM)] + [VMEM] * 8 + [ANY] * len(tokens),
        out_specs=[VMEM] * 11,
        compiler_params=pltpu.CompilerParams(vmem_limit_bytes=4 << 20),
        cost_estimate=SMALL,
        name="prepare",
    )(place, *routes, *saved, *new, *tokens)


def first_rows_kernel(rows, grads, out, held, sems):
    copies = [
        pltpu.make_async_copy(rows, held, sems.at[0]),
        pltpu.make_async_copy(grads, out.at[pl.ds(ROWS, ROWS)], sems.at[1]),
    ]
    for copy in copies:
        copy.start()
    copies[0].wait()
    v = held[...].astype(F32)
    out[:ROWS, :] = (v * lax.rsqrt(jnp.mean(v * v, axis=-1, keepdims=True) + EPS)).astype(BF16)
    copies[1].wait()


def first_rows(rows, grads):
    return pl.pallas_call(
        first_rows_kernel,
        out_shape=OUT(2 * ROWS, rows.shape[1]),
        in_specs=[ANY] * 2,
        out_specs=VMEM,
        scratch_shapes=[pltpu.VMEM(rows.shape, BF16), pltpu.SemaphoreType.DMA((2,))],
        compiler_params=pltpu.CompilerParams(vmem_limit_bytes=4 << 20),
        cost_estimate=SMALL,
        name="first_rows",
    )(in_hbm(rows), in_hbm(grads))


def pair_kernel(tokens, first, second, *refs):
    out, sems = refs[tokens:]
    copies = [
        pltpu.make_async_copy(first, out.at[pl.ds(0, first.shape[0])], sems.at[0]),
        pltpu.make_async_copy(second, out.at[pl.ds(first.shape[0], first.shape[0])], sems.at[1]),
    ]
    for copy in copies:
        copy.start()
    for copy in copies:
        copy.wait()


def pair(first, second, tokens):
    return pl.pallas_call(
        functools.partial(pair_kernel, len(tokens)),
        out_shape=OUT(2 * first.shape[0], first.shape[1]),
        in_specs=[ANY] * (2 + len(tokens)),
        out_specs=ANY,
        scratch_shapes=[pltpu.SemaphoreType.DMA((2,))],
        compiler_params=pltpu.CompilerParams(vmem_limit_bytes=1 << 20),
        cost_estimate=SMALL,
        name="pair",
    )(first, second, *tokens)


def tie_kernel(*refs):
    pass


def tie(value, tokens):
    return pl.pallas_call(
        tie_kernel,
        out_shape=jax.ShapeDtypeStruct(value.shape, value.dtype),
        in_specs=[ANY] * (1 + len(tokens)),
        out_specs=ANY,
        input_output_aliases={0: 0},
        compiler_params=pltpu.CompilerParams(vmem_limit_bytes=1 << 20),
        cost_estimate=SMALL,
        name="tie",
    )(value, *tokens)


def gather_near(own):
    return send(own, 0, 1), send(own, 2)


def gather_far(own, near, both):
    xp, y2 = near
    return own, xp, send(both, -1), y2, send(y2, 0, 1), send(both, 1)


def total(*parts):
    result = parts[0].astype(F32)
    for part in parts[1:]:
        result = result + part.astype(F32)
    return result


def reduce_far(pieces):
    return send(pieces[2], 1), send(pieces[5], -1), send(pieces[4], 0, 1)


def reduce_near(pieces, far):
    from_yp, from_ym, from_x = far
    to_x = total(pieces[1], from_yp[ROWS:], from_ym[ROWS:]).astype(BF16)
    to_y2 = total(pieces[3], from_x).astype(BF16)
    return (to_x, to_y2), (send(to_x, 0, 1), send(to_y2, 2))


def reduce_end(pieces, far, near):
    return total(pieces[0], far[0][:ROWS], far[1][:ROWS], near[0], near[1])


def normalize(v):
    v = v.astype(F32)
    return v * lax.rsqrt(jnp.mean(v * v, axis=-1, keepdims=True) + EPS)


def normal_back(x, cot):
    _, pull = jax.vjp(normalize, x.astype(F32))
    return pull(cot)[0]


def local(
    fwd_in,
    fwd_new,
    grad_in,
    grad_new,
    saved_x,
    saved_gate,
    saved_up,
    fwd_order,
    fwd_weight,
    bwd_order,
    bwd_weight,
    w_gate,
    w_up,
    w_down,
):
    columns = w_gate.shape[2]
    index = lax.axis_index("expert")
    y, x, core = index // (NX * NC), index // NC % NX, index % NC
    owner = index * columns // FF
    section_now = lax.axis_index("section")
    is_first = section_now == 0
    is_last = section_now == lax.axis_size("section") - 1

    place = jnp.stack([y, x, core, owner, is_first, is_last]).astype(jnp.int32)
    routes = [v[:, 0] for v in (fwd_order, fwd_weight, bwd_order, bwd_weight)]
    rows = first_rows(fwd_in[0], grad_in[0])
    near = gather_near(rows)
    prepared = prepare(place, routes, (saved_gate[:, 0], saved_up[:, 0]), (fwd_new, grad_new), (rows,))
    fwd_scale, bwd_scale, mine, others = prepared[:2], prepared[2:4], prepared[4:8], prepared[8]
    new_rows, new_grads = prepared[9:]

    weights = [w_gate[0], w_up[0], w_down[0]]
    own = hold(*weights, prepared[:1])
    theirs = send(others, 0, 0, 1)
    peer = hold(*[send(w, 0, 0, 1) for w in weights], prepared[:1])
    gates, gates_t, ups, ups_t, downs = map(list, zip(own, peer))
    both_shards = gather_far(rows, near, pair(rows, near[0], ()))

    def forward(shards, first, which, tokens=()):
        return layer(
            forward_kernel,
            "forward",
            shards,
            first,
            [fwd_scale[which]],
            [*gates, *ups, *downs],
            pltpu.VMEM((ROWS * NY * NX, 2 * columns), BF16),
            tokens,
        )

    def backward(shards, first, which, tokens=()):
        saved = [mine[which], mine[2 + which], theirs[which], theirs[2 + which]]
        return layer(
            backward_kernel,
            "backward",
            shards,
            first,
            [bwd_scale[which], *saved],
            [*gates_t, *ups_t, *downs],
            pltpu.VMEM((4, ROWS * NY * NX, columns), BF16),
            tokens,
        )

    def start(x_parts, g_shards, first, which):
        x_far = reduce_far(x_parts)
        g_parts = backward(g_shards, first, which, x_parts[:1])
        if which == 0:
            x_far = [tie(v, g_parts[:1]) for v in x_far]
            x_sent, x_close = reduce_near(x_parts, x_far)
            g_parts = [tie(v, x_sent) if k in (2, 4, 5) else v for k, v in enumerate(g_parts)]
            g_far = reduce_far(g_parts)
        else:
            g_far = reduce_far(g_parts)
            x_far = (tie(x_far[0], g_parts[:1]), *x_far[1:])
            _, x_close = reduce_near(x_parts, x_far)
        return reduce_end(x_parts, x_far, x_close), g_parts, g_far

    def finish(g_rows, which, g_parts, g_far, token):
        g_far = (tie(g_far[0], (token,)), *g_far[1:])
        _, g_close = reduce_near(g_parts, g_far)
        dxn = reduce_end(g_parts, g_far, g_close)
        return (g_rows.astype(F32) + normal_back(saved_x[which, 0], dxn)).astype(BF16)

    x_parts = forward(both_shards, 0, 0)
    x_sum, g_parts, g_far = start(x_parts, both_shards, 1, 0)
    first_out = (fwd_in[0].astype(F32) + x_sum).astype(BF16)
    x_rows = from_behind(first_out, "section", 1) + new_rows
    xn = normalize(x_rows).astype(BF16)
    first_grad = finish(grad_in[0], 0, g_parts, g_far, xn)
    g_rows = from_behind(first_grad, "section", -1) + new_grads
    x_near = gather_near(xn)
    x_both = pair(xn, x_near[0], ())
    x_shards = gather_far(xn, x_near, x_both)
    g_rows = tie(g_rows, (x_both, x_near[1]))
    g_near = gather_near(g_rows)
    g_both = pair(g_rows, g_near[0], (x_shards[4],))
    g_shards = gather_far(g_rows, g_near, g_both)
    x_parts = forward(x_shards, 0, 1)
    x_sum, g_parts, g_far = start(x_parts, g_shards, 0, 1)
    final_out = (x_rows.astype(F32) + x_sum).astype(BF16)
    final_grad = finish(g_rows, 1, g_parts, g_far, final_out)
    return (final_out[None], final_grad[None])


def solution(mesh):
    return jax.shard_map(
        local,
        mesh=mesh,
        in_specs=(
            P("section", "expert", None),
            P("expert", None),
            P("section", "expert", None),
            P("expert", None),
            P(None, "section", "expert", None),
            P(None, "section", None, "expert"),
            P(None, "section", None, "expert"),
            P(None, "section", None, None),
            P(None, "section", None, None),
            P(None, "section", None, None),
            P(None, "section", None, None),
            P("section", None, "expert"),
            P("section", None, "expert"),
            P("section", "expert", None),
        ),
        out_specs=(P("section", "expert", None), P("section", "expert", None)),
        check_vma=False,
    )
```

```python
import functools

import jax
import jax.numpy as jnp
from jax import lax
from jax.experimental import pallas as pl
from jax.experimental.pallas import tpu as pltpu
from jax.sharding import PartitionSpec as P

FF = 2048
EPS = 1e-06
BF16 = jnp.bfloat16
F32 = jnp.float32

NY, NX, NC = 4, 2, 2
ROWS = 16
TILE = 1024

PIECES = ((0, 1), (1, 1), (2, 2), (4, 1), (5, 1), (6, 2))

SMALL = pl.CostEstimate(flops=0, bytes_accessed=0, transcendentals=0)

ANY = pl.BlockSpec(memory_space=pl.ANY)
VMEM = pl.BlockSpec(memory_space=pltpu.VMEM)


def perm(dy, dx, dc):
    def at(y, x, c):
        return ((y % NY) * NX + x % NX) * NC + c % NC

    return [(at(y, x, c), at(y + dy, x + dx, c + dc)) for y in range(NY) for x in range(NX) for c in range(NC)]


def send(value, dy, dx=0, dc=0):
    return lax.ppermute(value, "expert", perm(dy, dx, dc))


def from_behind(value, axis, steps):
    count = lax.axis_size(axis)
    initial, last = (max(0, -steps), min(count, count - steps))
    return lax.ppermute(value, axis, [(source, source + steps) for source in range(initial, last)])


def dot(a, b):
    return jnp.dot(a, b, preferred_element_type=F32)


def dot_t(a, b):
    return lax.dot_general(a, b, (((1,), (1,)), ((), ())), preferred_element_type=F32)


def rows_of(piece):
    return slice(ROWS * piece[0], ROWS * (piece[0] + piece[1]))


def fill(full, shards, first):
    for shard, (block, blocks) in zip(shards, PIECES):
        stride = shard.shape[0] // (ROWS * blocks)
        for k in range(blocks):
            start = ROWS * (stride * k + first)
            full[ROWS * (block + k) : ROWS * (block + k + 1), :] = shard[start : start + ROWS, :]


def forward_kernel(tokens, first, *refs):
    shards, scale, gates, ups, downs = refs[:6], refs[6], refs[7:9], refs[9:11], refs[11:13]
    outs, (full, hidden) = refs[13 + tokens : 19 + tokens], refs[19 + tokens :]
    fill(full, shards, first)
    units = gates[0].shape[1]
    for i in range(2):
        gate = dot(full[...], gates[i][...])
        up = dot(full[...], ups[i][...])
        hidden[:, units * i : units * (i + 1)] = (scale[...] * (gate * jax.nn.sigmoid(gate)) * up).astype(BF16)
    for start in range(0, full.shape[1], TILE):
        cols = slice(start, start + TILE)
        part = dot(hidden[:, :units], downs[0][:, cols]) + dot(hidden[:, units:], downs[1][:, cols])
        part = part.astype(BF16)
        for out, piece in zip(outs, PIECES):
            out[:, cols] = part[rows_of(piece)]


def backward_kernel(tokens, first, *refs):
    shards, scale, saved, gates, ups, downs = refs[:6], refs[6], refs[7:11], refs[11:13], refs[13:15], refs[15:17]
    outs, (full, inner) = refs[17 + tokens : 23 + tokens], refs[23 + tokens :]
    fill(full, shards, first)
    units = gates[0].shape[1]
    for i in range(2):
        dh = dot_t(full[...], downs[i][...]) * scale[...]
        sg, su = saved[2 * i][...].astype(F32), saved[2 * i + 1][...].astype(F32)
        sig = jax.nn.sigmoid(sg)
        inner[2 * i] = (dh * su * (sig * (1.0 + sg * (1.0 - sig)))).astype(BF16)
        inner[2 * i + 1] = (dh * (sg * sig)).astype(BF16)
    weights = (gates[0], ups[0], gates[1], ups[1])
    for start in range(0, full.shape[1], TILE):
        cols = slice(start, start + TILE)
        part = dot(inner[0], weights[0][:, cols])
        for i in range(1, 4):
            part = part + dot(inner[i], weights[i][:, cols])
        part = part.astype(BF16)
        for out, piece in zip(outs, PIECES):
            out[:, cols] = part[rows_of(piece)]


def OUT(rows, width):
    return pltpu.VMEM((rows, width), BF16)


def in_vmem(value):
    return pltpu.with_memory_space_constraint(value, pltpu.VMEM)


def in_hbm(value):
    return pltpu.with_memory_space_constraint(value, pltpu.HBM)


def hold_kernel(gate, up, down, *refs):
    gate_out, gate_t, up_out, up_t, down_out, sems = refs[-6:]
    pairs = ((gate, gate_out), (up, up_out), (down, down_out))
    copies = [pltpu.make_async_copy(a, b, sems.at[i]) for i, (a, b) in enumerate(pairs)]
    for copy in copies:
        copy.start()
    for copy, whole, turned in ((copies[0], gate_out, gate_t), (copies[1], up_out, up_t)):
        copy.wait()
        for start in range(0, whole.shape[0], TILE):
            turned[:, start : start + TILE] = whole[start : start + TILE, :].T
    copies[2].wait()


def hold(gate, up, down, tokens):
    width, units = gate.shape
    tall, flat = pltpu.VMEM((width, units), BF16), pltpu.VMEM((units, width), BF16)
    return pl.pallas_call(
        hold_kernel,
        out_shape=[tall, flat, tall, flat, flat],
        in_specs=[ANY] * (3 + len(tokens)),
        out_specs=[VMEM] * 5,
        scratch_shapes=[pltpu.SemaphoreType.DMA((3,))],
        compiler_params=pltpu.CompilerParams(vmem_limit_bytes=2 << 20),
        cost_estimate=SMALL,
        name="hold",
    )(in_hbm(gate), in_hbm(up), in_hbm(down), *tokens)


def layer(kernel, name, shards, first, small, weights, scratch, tokens):
    width = weights[-1].shape[1]
    count = ROWS * NY * NX
    units = weights[-1].shape[0]
    operands = [*map(in_vmem, shards), *small, *map(in_vmem, weights)]
    return pl.pallas_call(
        functools.partial(kernel, len(tokens), first),
        out_shape=[OUT(ROWS * blocks, width) for _, blocks in PIECES],
        in_specs=[VMEM] * len(operands) + [ANY] * len(tokens),
        out_specs=[VMEM] * 6,
        scratch_shapes=[pltpu.VMEM((count, width), BF16), scratch],
        compiler_params=pltpu.CompilerParams(vmem_limit_bytes=4 << 20),
        cost_estimate=SMALL,
        name=name,
    )(*operands, *tokens)


def prepare_kernel(
    tokens, place, fwd_order, fwd_weight, bwd_order, bwd_weight, saved_gate, saved_up, fwd_new, grad_new, *refs
):
    outs, tall = refs[tokens:-1], refs[-1]
    scales, mine, others = outs[:4], outs[4:8], outs[8]
    outs[9][...] = jnp.where(place[4] == 1, fwd_new[...], jnp.zeros_like(fwd_new))
    outs[10][...] = jnp.where(place[5] == 1, grad_new[...], jnp.zeros_like(grad_new))
    y, x, core, owner = (place[i] for i in range(4))
    for which in range(2):
        for i, (order, weight) in enumerate(((fwd_order, fwd_weight), (bwd_order, bwd_weight))):
            o, w = order[which], weight[which]
            column = jnp.where(owner == 0, o[:1], o[1:])
            scale = jnp.where(column == 0, w[:1], w[1:])
            tall[2 * i + which] = jnp.broadcast_to(scale, (tall.shape[2], scale.shape[1])).T
    for k in range(NY * NX):
        chip = lax.rem(y + k // NX, NY) * NX + lax.rem(x + k % NX, NX)
        rows = slice(ROWS * k, ROWS * (k + 1))
        here = pl.ds(pl.multiple_of((chip * NC + core) * ROWS, ROWS), ROWS)
        there = pl.ds(pl.multiple_of((chip * NC + 1 - core) * ROWS, ROWS), ROWS)
        for which in range(2):
            for i in range(2):
                scales[2 * i + which][rows, :] = tall[2 * i + which, here, :1]
            for i, saved in enumerate((saved_gate, saved_up)):
                mine[2 * i + which][rows, :] = saved[which, here, :]
                others[2 * i + which, rows, :] = saved[which, there, :]


def prepare(place, routes, saved, new, tokens):
    count, units = ROWS * NY * NX, saved[0].shape[2]
    return pl.pallas_call(
        functools.partial(prepare_kernel, len(tokens)),
        out_shape=[jax.ShapeDtypeStruct((count, 1), F32)] * 4
        + [jax.ShapeDtypeStruct((count, units), BF16)] * 4
        + [jax.ShapeDtypeStruct((4, count, units), BF16)]
        + [jax.ShapeDtypeStruct(v.shape, BF16) for v in new],
        in_specs=[pl.BlockSpec(memory_space=pltpu.SMEM)] + [VMEM] * 8 + [ANY] * len(tokens),
        out_specs=[VMEM] * 11,
        scratch_shapes=[pltpu.VMEM((4, saved[0].shape[1], 128), F32)],
        compiler_params=pltpu.CompilerParams(vmem_limit_bytes=4 << 20),
        cost_estimate=SMALL,
        name="prepare",
    )(place, *routes, *saved, *new, *tokens)


def first_rows_kernel(rows, grads, place, out, held, sems):
    copies = [
        pltpu.make_async_copy(rows, held, sems.at[0]),
        pltpu.make_async_copy(grads, out.at[pl.ds(ROWS, ROWS)], sems.at[1]),
    ]
    for copy in copies:
        copy.start()
    copies[0].wait()
    v = held[...].astype(F32)
    out[:ROWS, :] = (v * lax.rsqrt(jnp.mean(v * v, axis=-1, keepdims=True) + EPS)).astype(BF16)
    copies[1].wait()


def first_rows(rows, grads, place):
    return pl.pallas_call(
        first_rows_kernel,
        out_shape=OUT(2 * ROWS, rows.shape[1]),
        in_specs=[ANY] * 3,
        out_specs=VMEM,
        scratch_shapes=[pltpu.VMEM(rows.shape, BF16), pltpu.SemaphoreType.DMA((2,))],
        compiler_params=pltpu.CompilerParams(vmem_limit_bytes=4 << 20),
        cost_estimate=SMALL,
        name="first_rows",
    )(in_hbm(rows), in_hbm(grads), place)


def pair_kernel(tokens, first, second, *refs):
    out, sems = refs[tokens:]
    copies = [
        pltpu.make_async_copy(first, out.at[pl.ds(0, first.shape[0])], sems.at[0]),
        pltpu.make_async_copy(second, out.at[pl.ds(first.shape[0], first.shape[0])], sems.at[1]),
    ]
    for copy in copies:
        copy.start()
    for copy in copies:
        copy.wait()


def pair(first, second, tokens):
    return pl.pallas_call(
        functools.partial(pair_kernel, len(tokens)),
        out_shape=OUT(2 * first.shape[0], first.shape[1]),
        in_specs=[ANY] * (2 + len(tokens)),
        out_specs=ANY,
        scratch_shapes=[pltpu.SemaphoreType.DMA((2,))],
        compiler_params=pltpu.CompilerParams(vmem_limit_bytes=1 << 20),
        cost_estimate=SMALL,
        name="pair",
    )(first, second, *tokens)


def tie_kernel(*refs):
    pass


def tie(value, tokens):
    return pl.pallas_call(
        tie_kernel,
        out_shape=jax.ShapeDtypeStruct(value.shape, value.dtype),
        in_specs=[ANY] * (1 + len(tokens)),
        out_specs=ANY,
        input_output_aliases={0: 0},
        compiler_params=pltpu.CompilerParams(vmem_limit_bytes=1 << 20),
        cost_estimate=SMALL,
        name="tie",
    )(value, *tokens)


def gather_near(own):
    return send(own, 0, 1), send(own, 2)


def gather_far(own, near, both):
    xp, y2 = near
    return own, xp, send(both, -1), y2, send(y2, 0, 1), send(both, 1)


def total(*parts):
    result = parts[0].astype(F32)
    for part in parts[1:]:
        result = result + part.astype(F32)
    return result


def reduce_far(pieces):
    return send(pieces[2], 1), send(pieces[5], -1), send(pieces[4], 0, 1)


def reduce_near(pieces, far):
    from_yp, from_ym, from_x = far
    to_x = total(pieces[1], from_yp[ROWS:], from_ym[ROWS:]).astype(BF16)
    to_y2 = total(pieces[3], from_x).astype(BF16)
    return (to_x, to_y2), (send(to_x, 0, 1), send(to_y2, 2))


def reduce_end(pieces, far, near):
    return total(pieces[0], far[0][:ROWS], far[1][:ROWS], near[0], near[1])


def normalize(v):
    v = v.astype(F32)
    return v * lax.rsqrt(jnp.mean(v * v, axis=-1, keepdims=True) + EPS)


def normal_back(x, cot):
    _, pull = jax.vjp(normalize, x.astype(F32))
    return pull(cot)[0]


def local(
    fwd_in,
    fwd_new,
    grad_in,
    grad_new,
    saved_x,
    saved_gate,
    saved_up,
    fwd_order,
    fwd_weight,
    bwd_order,
    bwd_weight,
    w_gate,
    w_up,
    w_down,
):
    columns = w_gate.shape[2]
    index = lax.axis_index("expert")
    y, x, core = index // (NX * NC), index // NC % NX, index % NC
    owner = index * columns // FF
    section_now = lax.axis_index("section")
    is_first = section_now == 0
    is_last = section_now == lax.axis_size("section") - 1

    place = jnp.stack([y, x, core, owner, is_first, is_last]).astype(jnp.int32)
    routes = [v[:, 0].transpose(0, 2, 1) for v in (fwd_order, fwd_weight, bwd_order, bwd_weight)]
    rows = first_rows(fwd_in[0], grad_in[0], place)
    near = gather_near(rows)
    prepared = prepare(place, routes, (saved_gate[:, 0], saved_up[:, 0]), (fwd_new, grad_new), (rows,))
    fwd_scale, bwd_scale, mine, others = prepared[:2], prepared[2:4], prepared[4:8], prepared[8]
    new_rows, new_grads = prepared[9:]

    weights = [w_gate[0], w_up[0], w_down[0]]
    own = hold(*weights, prepared[:1])
    theirs = send(others, 0, 0, 1)
    peer = hold(*[send(w, 0, 0, 1) for w in weights], prepared[:1])
    gates, gates_t, ups, ups_t, downs = map(list, zip(own, peer))
    both_shards = gather_far(rows, near, pair(rows, near[0], ()))

    def forward(shards, first, which, tokens=()):
        return layer(
            forward_kernel,
            "forward",
            shards,
            first,
            [fwd_scale[which]],
            [*gates, *ups, *downs],
            pltpu.VMEM((ROWS * NY * NX, 2 * columns), BF16),
            tokens,
        )

    def backward(shards, first, which, tokens=()):
        saved = [mine[which], mine[2 + which], theirs[which], theirs[2 + which]]
        return layer(
            backward_kernel,
            "backward",
            shards,
            first,
            [bwd_scale[which], *saved],
            [*gates_t, *ups_t, *downs],
            pltpu.VMEM((4, ROWS * NY * NX, columns), BF16),
            tokens,
        )

    def grads(g_rows, which, dxn):
        return (g_rows.astype(F32) + normal_back(saved_x[which, 0], dxn)).astype(BF16)

    def follow(x_parts, x_far, token):
        x_far = (tie(x_far[0], (token,)), *x_far[1:])
        _, x_close = reduce_near(x_parts, x_far)
        return reduce_end(x_parts, x_far, x_close)

    g_parts = backward(both_shards, 1, 0)
    g_far = reduce_far(g_parts)
    x_parts = forward(both_shards, 0, 0, g_parts[:1])
    g_far = [tie(v, x_parts[:1]) for v in g_far]
    g_sent, g_close = reduce_near(g_parts, g_far)
    x_parts = [tie(v, g_sent) if k in (2, 4, 5) else v for k, v in enumerate(x_parts)]
    x_far = reduce_far(x_parts)
    first_grad = grads(grad_in[0], 0, reduce_end(g_parts, g_far, g_close))
    g_rows = from_behind(first_grad, "section", -1) + new_grads
    first_out = (fwd_in[0].astype(F32) + follow(x_parts, x_far, g_rows)).astype(BF16)
    x_rows = from_behind(first_out, "section", 1) + new_rows

    g_near = gather_near(g_rows)
    g_both = pair(g_rows, g_near[0], ())
    g_shards = gather_far(g_rows, g_near, g_both)
    xn = tie(normalize(x_rows).astype(BF16), (g_both, g_near[1]))
    x_near = gather_near(xn)
    x_both = pair(xn, x_near[0], (g_shards[4],))
    x_shards = gather_far(xn, x_near, x_both)
    g_parts = backward(g_shards, 0, 1)
    g_far = reduce_far(g_parts)
    x_parts = forward(x_shards, 0, 1, g_parts[:1])
    x_far = reduce_far(x_parts)
    g_far = (tie(g_far[0], x_parts[:1]), *g_far[1:])
    _, g_close = reduce_near(g_parts, g_far)
    final_grad = grads(g_rows, 1, reduce_end(g_parts, g_far, g_close))
    final_out = (x_rows.astype(F32) + follow(x_parts, x_far, final_grad)).astype(BF16)
    return (final_out[None], final_grad[None])


def solution(mesh):
    return jax.shard_map(
        local,
        mesh=mesh,
        in_specs=(
            P("section", "expert", None),
            P("expert", None),
            P("section", "expert", None),
            P("expert", None),
            P(None, "section", "expert", None),
            P(None, "section", None, "expert"),
            P(None, "section", None, "expert"),
            P(None, "section", None, None),
            P(None, "section", None, None),
            P(None, "section", None, None),
            P(None, "section", None, None),
            P("section", None, "expert"),
            P("section", None, "expert"),
            P("section", "expert", None),
        ),
        out_specs=(P("section", "expert", None), P("section", "expert", None)),
        check_vma=False,
    )
```
